32 devices in a mesh: map: 2 (over x), rows: 16 (over z, y, core).
Axes of the slice: x: 2, y: 2, z: 4, core: 2. Of those that a mesh axis runs over, the one named last changes fastest.
Arguments:
- density: bfloat16 [16, 2048, 2048], P('map', 'rows'), parts along dimension 0, may hold values from 0 to 2300, as said below
- lens_weight: float32 [8], replicated, may hold values from 0.05 to 0.5
- bin_distance: float32 [16], replicated, may hold values from 0.5 to 2.5, as said below
- plane_bin: int32 [8], replicated, may hold values from 0 to 15, as said below
- source_plane: int32 [1], replicated, may hold values from 1 to 7, as said below
Outputs:
- shear: float32 [2, 2, 2048, 2048], P('map', None, 'rows'), parts along dimension 0
The draws below stay inside these ranges and needn't reach their ends.
There are 2 independent parts, one for each index of `map`. The reference program is written for one: setup_inputs(seed, part) draws one part's arguments, and reference() takes and returns one part's arrays. A program takes and returns all parts, laid end to end along the dimension named above; an argument that names none is the same for every part. Nothing has to cross between parts.
Inputs may be any that keep to these rules, and one draw needn't show every extreme that they name: `density`: positive. `bin_distance`: increasing. `plane_bin`: strictly increasing over the planes. `source_plane`: distinct and increasing.
All inputs are finite; a program needn't handle non-finite values.
Results may differ from the reference program's by a relative error of at most 0.0003.
Values sent between devices are 32-bit elements; how exact they have to be, the bound alone decides.
A program may use at most 64 MiB of HBM per device.

```python
import math
import jax
import jax.numpy as jnp
from jax import lax

NX = 2048
NY = 2048
PLANES = 8
SOURCES = 1
NBINS = 16


def draw_density(key, part):
    key_rows, key_cols, key_planes, key_base = jax.random.split(key, 4)
    rows_frac = jnp.arange(NX, dtype=jnp.float32) / NX
    row_power = 0.5 * rows_frac + 0.5 * jax.random.uniform(key_rows, (NX,), dtype=jnp.float32)
    col_power = jax.random.uniform(key_cols, (NY,), dtype=jnp.float32)
    plane_power = jax.random.uniform(key_planes, (PLANES,), dtype=jnp.float32, minval=-0.3, maxval=0.3)
    normals = jnp.clip(jax.random.normal(key_base, (PLANES, NX, NY), dtype=jnp.float32), -4.0, 4.0)
    base = jnp.exp(0.6 * normals)
    power = row_power[None, :, None] + col_power[None, None, :] + plane_power[:, None, None]
    return (base * jnp.power(10.0, power)).astype(jnp.bfloat16)


def draw_bin_distance(key, part):
    steps_drawn = jax.random.uniform(key, (NBINS,), dtype=jnp.float32, minval=0.5, maxval=1.5)
    running = jnp.cumsum(steps_drawn) - steps_drawn[0]
    return 0.5 + 2.0 * running / running[NBINS - 1]


def draw_plane_bin(key, part):
    inner = jax.random.permutation(key, NBINS - 2)[:PLANES - 2].astype(jnp.int32) + 1
    chosen = jnp.concatenate([jnp.zeros((1,), jnp.int32), inner, jnp.full((1,), NBINS - 1, jnp.int32)])
    return jnp.sort(chosen)


def draw_source_plane(key, part):
    inner = jax.random.permutation(key, PLANES - 2)[:SOURCES - 1].astype(jnp.int32) + 1
    chosen = jnp.concatenate([inner, jnp.full((1,), PLANES - 1, jnp.int32)])
    return jnp.sort(chosen)


def setup_inputs(seed: int = 0, part: int = 0) -> dict:
    key_of = jax.random.split(jax.random.key(seed), 6)
    part_splits = jax.random.split(jax.random.fold_in(key_of[5], part), 6)
    density = draw_density(jax.random.fold_in(jax.random.fold_in(key_of[5], part), 71), part)
    lens_weight = jnp.clip(jnp.exp(jax.random.uniform(key_of[1], (PLANES,), jnp.float32, math.log(0.05), math.log(0.5))), 0.05, 0.5)
    bin_distance = draw_bin_distance(jax.random.fold_in(key_of[5], 71), part)
    plane_bin = draw_plane_bin(jax.random.fold_in(key_of[5], 71), part)
    source_plane = draw_source_plane(jax.random.fold_in(key_of[5], 71), part)
    return {"density": density, "lens_weight": lens_weight, "bin_distance": bin_distance, "plane_bin": plane_bin, "source_plane": source_plane}


def signed_frequency(positions, length):
    return jnp.where(positions < length // 2, positions, positions - length).astype(jnp.float32) / length


def shear_kernel(row_positions, col_positions, total_rows, total_cols):
    wave_rows = signed_frequency(row_positions, total_rows)[:, None]
    wave_cols = signed_frequency(col_positions, total_cols)[None, :]
    squared = wave_rows * wave_rows + wave_cols * wave_cols
    denominator = jnp.where(squared > 0, squared, jnp.float32(1.0))
    return (wave_rows * wave_rows - wave_cols * wave_cols) / denominator, 2.0 * wave_rows * wave_cols / denominator


def lens_coefficients(lens_weight, bin_distance, plane_bin, source_plane):
    bin_ids = jnp.arange(bin_distance.shape[0], dtype=jnp.int32)
    distance = jnp.sum(jnp.where(plane_bin[:, None] == bin_ids[None, :], bin_distance[None, :], jnp.float32(0.0)), axis=1)
    planes = jnp.arange(plane_bin.shape[0], dtype=jnp.int32)
    picked = source_plane[:, None] == planes[None, :]
    source_distance = jnp.sum(jnp.where(picked, distance[None, :], jnp.float32(0.0)), axis=1)
    nearer = planes[None, :] <= source_plane[:, None]
    weights = lens_weight[None, :] * (1.0 - distance[None, :] / source_distance[:, None])
    return jnp.where(nearer, weights, jnp.float32(0.0))


def reference(density, lens_weight, bin_distance, plane_bin, source_plane):
    total_rows = density.shape[1]
    total_cols = density.shape[2]
    plane_mean = jnp.sum(density.astype(jnp.float32), axis=(1, 2)) / (total_rows * total_cols)
    contrast = density.astype(jnp.float32) / plane_mean[:, None, None] - 1.0
    coefficients = lens_coefficients(lens_weight, bin_distance, plane_bin, source_plane)
    convergence = jnp.einsum('sl,lxy->sxy', coefficients, contrast, precision=lax.Precision.HIGHEST)
    spectrum = jnp.fft.fft2(convergence, axes=(1, 2))
    kernel_plus, kernel_cross = shear_kernel(jnp.arange(total_rows, dtype=jnp.int32), jnp.arange(total_cols, dtype=jnp.int32), total_rows, total_cols)
    sheared = lax.complex(kernel_plus, kernel_cross)[None] * spectrum
    returned = jnp.fft.ifft2(sheared, axes=(1, 2))
    return jnp.stack([jnp.real(returned), jnp.imag(returned)], axis=1)
```

```python
import functools

import jax
import jax.numpy as jnp
import ml_dtypes
import numpy as np
from jax import lax
from jax.experimental import pallas as pl
from jax.experimental.pallas import tpu as pltpu
from jax.sharding import PartitionSpec as P

RADIX = 16
GROUP = RADIX // 2
ROWS16 = 16
MESH = pl.DeviceIdType.MESH
F32 = jnp.float32
BF16 = jnp.bfloat16


def split_table(table):
    high = table.astype(ml_dtypes.bfloat16)
    low = (table - high.astype(np.float64)).astype(ml_dtypes.bfloat16)
    return np.stack([high, low], axis=1)


def column_tables(total_rows, total_cols):
    block = total_cols // RADIX
    half = block // 2
    inside = np.arange(block)
    forward = np.zeros((GROUP, 2 * block, 2 * block))
    inverse = np.zeros((GROUP, 2 * block, 2 * block))
    for j in range(GROUP):
        for c in range(2):
            k = c * half + np.arange(half)
            freq = GROUP * k if j == 0 else j + RADIX * k
            angle = 2 * np.pi * ((inside[:, None] * freq[None, :]) % total_cols) / total_cols
            cos, sin = np.cos(angle), np.sin(angle)
            real = slice(c * block, c * block + half)
            imag = slice(c * block + half, (c + 1) * block)
            if j == 0:
                even = (k % 2 == 0)[None, :]
                cos_both = np.concatenate([np.where(even, cos, 0.0), np.where(even, 0.0, cos)])
                sin_both = np.concatenate([np.where(even, sin, 0.0), np.where(even, 0.0, sin)])
                fwd_re, fwd_im = cos_both, -sin_both
                inv_re, inv_im = 2 * cos_both, -2 * sin_both
                if c == 0:
                    sign = np.concatenate([(-1.0) ** inside, np.zeros(block)])
                    fwd_im[:, 0] = sign
                    inv_re[:, 0] = cos_both[:, 0]
                    inv_im[:, 0] = sign
            else:
                fwd_re = np.concatenate([cos, sin])
                fwd_im = np.concatenate([-sin, cos])
                inv_re = np.concatenate([cos, sin])
                inv_im = np.concatenate([-sin, cos])
            forward[j][:, real] = fwd_re
            forward[j][:, imag] = fwd_im
            inverse[j][real, :] = inv_re.T
            inverse[j][imag, :] = inv_im.T
    return split_table(forward), split_table(inverse / (total_rows * total_cols))


def row_tables(total_rows):
    block = total_rows // RADIX
    inside = np.arange(block)
    forward, inverse = [], []
    for k1 in range(RADIX):
        freq = k1 + RADIX * inside
        angle = 2 * np.pi * ((freq[:, None] * inside[None, :]) % total_rows) / total_rows
        cos, sin = np.cos(angle), np.sin(angle)
        forward.append(np.concatenate([cos, -sin], axis=1))
        inverse.append(np.concatenate([cos.T, sin.T], axis=1))
    return split_table(np.stack(forward)), split_table(np.stack(inverse))


def scaled(number, value):
    return value if number == 1.0 else (-value if number == -1.0 else value * np.float32(number))


def plus_of(a, b):
    return b if a is None else (a if b is None else a + b)


def minus_of(a, b):
    return a if b is None else (-b if a is None else a - b)


def rotate(value, step, length, orient):
    re, im = value
    if step == 0:
        return value
    cos, sin = np.cos(2 * np.pi * step / length), orient * np.sin(2 * np.pi * step / length)
    if 4 * step == length:
        return (None if im is None else -sin * im, sin * re)
    if im is None:
        return (re * np.float32(cos), re * np.float32(sin))
    return (
        re * np.float32(cos) - im * np.float32(sin),
        re * np.float32(sin) + im * np.float32(cos),
    )


def real_forward(values):
    n = len(values)
    if n == 1:
        return [(values[0], None)]
    even, odd = real_forward(values[0::2]), real_forward(values[1::2])
    out = [None] * (n // 2 + 1)
    for k in range(n // 4 + 1):
        turned = rotate(odd[k], k, n, -1.0)
        out[k] = (plus_of(even[k][0], turned[0]), plus_of(even[k][1], turned[1]))
        other = minus_of(turned[1], even[k][1])
        out[n // 2 - k] = (minus_of(even[k][0], turned[0]), other)
        if 4 * k == n:
            out[k] = (even[k][0], minus_of(None, odd[k][0]))
    return out


def real_inverse(values):
    n = 2 * (len(values) - 1)
    if n == 2:
        a, b = values[0][0], values[1][0]
        return [a + b, a - b]
    even, odd = [], []
    for k in range(n // 4 + 1):
        a, b = values[k], values[n // 2 - k]
        if k == 0 or 4 * k == n:
            if k == 0:
                even.append((a[0] + b[0], None))
                odd.append((a[0] - b[0], None))
            else:
                even.append((2.0 * a[0], None))
                odd.append((-2.0 * a[1], None))
            continue
        even.append((a[0] + b[0], a[1] - b[1]))
        odd.append(rotate((a[0] - b[0], a[1] + b[1]), k, n, 1.0))
    out = [None] * n
    out[0::2] = real_inverse(even)
    out[1::2] = real_inverse(odd)
    return out


def times_i(value, sign):
    return pltpu.roll(value, value.shape[1] // 2, 1) * sign


def packed_dft(values, orient, sign):
    n = len(values)
    if n == 1:
        return values
    even, odd = packed_dft(values[0::2], orient, sign), packed_dft(values[1::2], orient, sign)
    out = [None] * n
    for k in range(n // 2):
        value = odd[k]
        if 4 * k == n:
            value = times_i(value, sign) * np.float32(orient)
        elif k:
            angle = 2 * np.pi * k / n
            value = value * np.float32(np.cos(angle)) + times_i(value, sign) * np.float32(
                orient * np.sin(angle)
            )
        out[k] = even[k] + value
        out[k + n // 2] = even[k] - value
    return out


def halves(value):
    high = value.astype(BF16)
    return high, (value - high.astype(F32)).astype(BF16)


def product(a, b):
    def dot(x, y):
        return jnp.dot(x, y, preferred_element_type=F32)

    return dot(a[0], b[0]) + dot(a[0], b[1]) + dot(a[1], b[0])


def frequency(positions, length):
    return jnp.where(positions < length // 2, positions, positions - length).astype(F32) / length


def kernel(
    n, density, weight, bins, plane_bin, source, col_fwd, col_inv, row_fwd, row_inv, out,
    dens, tab_cf, tab_ci, tab_rf, tab_ri, part, sums, parts, sbuf, xin, zbuf, zconj, wbuf, gbuf,
    rbuf, acc, load_sem, send_m, recv_m, send_f, recv_f, send_r, recv_r, own_sem,
):
    planes, rows, cols = density.shape
    total_rows = rows * n
    block = cols // RADIX
    half = block // 2
    xblock = total_rows // RADIX
    me = lax.axis_index("rows")
    group = me // GROUP
    mine = me % GROUP

    loads = [pltpu.make_async_copy(density.at[l], dens.at[l], load_sem.at[l]) for l in range(planes)]
    for at, (src, dst) in enumerate(
        [(col_fwd, tab_cf), (row_fwd, tab_rf), (row_inv, tab_ri), (col_inv, tab_ci)]
    ):
        loads.append(pltpu.make_async_copy(src, dst, load_sem.at[planes + at]))
    for load in loads:
        load.start()

    barrier = pltpu.get_barrier_semaphore()

    @pl.loop(1, n)
    def _(off):
        pl.semaphore_signal(
            barrier, inc=1, device_id={"rows": (me + off) % n}, device_id_type=MESH
        )

    for l in range(planes):
        loads[l].wait()

        def add_rows(i, total, l=l):
            at = pl.ds(pl.multiple_of(i * ROWS16, ROWS16), ROWS16)
            pieces = [dens[l, at, a * block:(a + 1) * block].astype(F32) for a in range(RADIX)]
            while len(pieces) > 1:
                pieces = [x + y for x, y in zip(pieces[0::2], pieces[1::2])]
            return total + pieces[0]

        total = lax.fori_loop(0, rows // ROWS16, add_rows, jnp.zeros((ROWS16, block), F32))
        part[l:l + 1, :] = jnp.sum(total, axis=0, keepdims=True)

    pl.semaphore_wait(barrier, n - 1)

    def sums_copy(dst, slot):
        return pltpu.make_async_remote_copy(
            src_ref=part, dst_ref=sums.at[slot], send_sem=send_m.at[dst], recv_sem=recv_m.at[slot],
            device_id={"rows": dst}, device_id_type=MESH,
        )

    @pl.loop(1, n)
    def _(off):
        sums_copy((me + off) % n, me).start()

    sums[me] = part[...]

    @pl.loop(1, n)
    def _(off):
        sums_copy((me + off) % n, (me + off) % n).wait_recv()

    cells = np.float32(total_rows * cols)
    whole = jnp.sum(jnp.sum(sums[...], axis=0), axis=1, keepdims=True)
    mean = jnp.broadcast_to(whole / cells, (planes, block))
    source_plane = source[0]
    source_distance = jnp.full((1, block), bins[plane_bin[source_plane]], F32)
    scales, offset = [], None
    for l in range(planes):
        distance = jnp.full((1, block), bins[plane_bin[l]], F32)
        lens = jnp.full((1, block), jnp.where(l <= source_plane, weight[l], np.float32(0.0)), F32)
        coefficient = lens * (1.0 - distance / source_distance)
        scales.append(coefficient / mean[l:l + 1, :])
        offset = coefficient if offset is None else offset + coefficient

    @pl.loop(0, rows // ROWS16)
    def _(i):
        at = pl.ds(pl.multiple_of(i * ROWS16, ROWS16), ROWS16)
        values = []
        for a in range(RADIX):
            value = None
            for l in range(planes):
                term = dens[l, at, a * block:(a + 1) * block].astype(F32) * scales[l]
                value = term if value is None else value + term
            values.append(value - offset)
        spectrum = real_forward(values)
        parts[0, at, :block] = spectrum[0][0]
        parts[0, at, block:] = spectrum[GROUP][0]
        for j in range(1, GROUP):
            parts[j, at, :block] = spectrum[j][0]
            parts[j, at, block:] = spectrum[j][1]

    loads[planes].wait()

    def forward_copy(c, dst, slot):
        return pltpu.make_async_remote_copy(
            src_ref=sbuf.at[c, dst % GROUP],
            dst_ref=xin.at[c, pl.ds(pl.multiple_of(slot * rows, rows), rows)],
            send_sem=send_f.at[c, dst], recv_sem=recv_f.at[c, slot],
            device_id={"rows": dst}, device_id_type=MESH,
        )

    def forward_own(c):
        return pltpu.make_async_copy(
            sbuf.at[c, mine], xin.at[c, pl.ds(pl.multiple_of(me * rows, rows), rows)],
            own_sem.at[c],
        )

    for c in range(2):
        lanes = slice(c * block, (c + 1) * block)

        @pl.loop(0, GROUP)
        def _(j, c=c, lanes=lanes):
            sbuf[c, j] = product(halves(parts[j]), (tab_cf[j, 0, :, lanes], tab_cf[j, 1, :, lanes]))

        forward_own(c).start()

        @pl.loop(1, n)
        def _(off, c=c):
            forward_copy(c, (me + off) % n, me).start()

    lane = lax.broadcasted_iota(jnp.int32, (1, block), 1)
    sign = jnp.where(lane < half, np.float32(-1.0), np.float32(1.0))
    loads[planes + 1].wait()
    loads[planes + 2].wait()
    loads[planes + 3].wait()

    def return_copy(c, dst, slot):
        return pltpu.make_async_remote_copy(
            src_ref=gbuf.at[c, :, pl.ds(pl.multiple_of(dst * rows, rows), rows)],
            dst_ref=rbuf.at[c, slot],
            send_sem=send_r.at[c, dst % GROUP], recv_sem=recv_r.at[c, slot],
            device_id={"rows": dst}, device_id_type=MESH,
        )

    def return_own(c):
        return pltpu.make_async_copy(
            gbuf.at[c, :, pl.ds(pl.multiple_of(me * rows, rows), rows)], rbuf.at[c, mine],
            own_sem.at[2 + c],
        )

    def peer(off):
        return group * GROUP + (mine + off) % GROUP

    for c in range(2):
        forward_own(c).wait()

        @pl.loop(1, n)
        def _(off, c=c):
            forward_copy(c, (me + off) % n, (me + off) % n).wait_recv()

        def first_pass(target, conjugate, c=c):
            @pl.loop(0, xblock // ROWS16)
            def _(i):
                at = pl.multiple_of(i * ROWS16, ROWS16)
                values = [xin[c, pl.ds(at + a * xblock, ROWS16), :] for a in range(RADIX)]
                if conjugate:
                    values = [-sign * value for value in values]
                for k1, value in enumerate(packed_dft(values, -1.0, sign)):
                    target[k1, pl.ds(at, ROWS16), :] = value

        first_pass(zbuf, False)
        if c == 0:
            first_pass(zconj, True)

        @pl.loop(0, RADIX)
        def _(k1, c=c):
            def transform(value):
                stacked = jnp.concatenate([value, times_i(value, sign)], axis=0)
                return product((tab_rf[k1, 0], tab_rf[k1, 1]), halves(stacked))

            spectrum = transform(zbuf[k1])
            turned = times_i(spectrum, sign)
            shape = (xblock, block)
            kx = k1 + RADIX * lax.broadcasted_iota(jnp.int32, shape, 0)
            q = lax.broadcasted_iota(jnp.int32, shape, 1) % half
            k2 = c * half + q
            ky = jnp.where(mine == 0, GROUP * k2, mine + RADIX * k2)
            fx, fy = frequency(kx, total_rows), frequency(ky, cols)
            squared = fx * fx + fy * fy
            recip = 1.0 / jnp.where(squared > 0, squared, np.float32(1.0))
            plus = (fx * fx - fy * fy) * recip
            cross = 2.0 * fx * fy * recip
            nyquist = kx == total_rows // 2
            zero = jnp.zeros(shape, F32)
            direct, across = plus, jnp.where(nyquist, cross, zero)
            second = jnp.where(nyquist, zero, cross) * spectrum
            if c == 0:
                mirrored = transform(zconj[k1])
                packed = jnp.logical_and(q == 0, mine == 0)
                recip_n = 1.0 / (fx * fx + np.float32(0.25))
                plus_n = (fx * fx - np.float32(0.25)) * recip_n
                cross_n = -fx * recip_n
                odd_n = jnp.where(nyquist, zero, cross_n)
                even_n = jnp.where(nyquist, cross_n, zero)
                mirror_direct = jnp.where(packed, 0.5 * (plus - plus_n), zero)
                mirror_across = jnp.where(packed, -0.5 * odd_n, zero)
                direct = jnp.where(packed, 0.5 * (plus + plus_n), direct)
                across = jnp.where(packed, 0.5 * odd_n, across)
                second = jnp.where(packed, 0.5 * even_n * (spectrum - mirrored), second)
                first = (
                    direct * spectrum + across * turned
                    + mirror_direct * mirrored + mirror_across * times_i(mirrored, sign)
                )
            else:
                first = direct * spectrum + across * turned
            both = jnp.concatenate(
                [
                    jnp.concatenate([first, times_i(first, sign)], axis=0),
                    jnp.concatenate([second, times_i(second, sign)], axis=0),
                ],
                axis=1,
            )
            wbuf[k1] = product((tab_ri[k1, 0], tab_ri[k1, 1]), halves(both))

        @pl.loop(0, xblock // ROWS16)
        def _(i, c=c):
            at = pl.multiple_of(i * ROWS16, ROWS16)
            for f in range(2):
                values = [
                    wbuf[k1, pl.ds(at, ROWS16), f * block:(f + 1) * block] for k1 in range(RADIX)
                ]
                for a, value in enumerate(packed_dft(values, 1.0, sign)):
                    gbuf[c, f, pl.ds(at + a * xblock, ROWS16), :] = value

        return_own(c).start()

        @pl.loop(1, GROUP)
        def _(off, c=c):
            return_copy(c, peer(off), mine).start()

    for c in range(2):
        return_own(c).wait()

        @pl.loop(1, GROUP)
        def _(off, c=c):
            return_copy(c, peer(off), (mine + off) % GROUP).wait_recv()

        rows_of = slice(c * block, (c + 1) * block)

        @pl.loop(0, GROUP)
        def _(j, c=c, rows_of=rows_of):
            for f in range(2):
                value = product(
                    halves(rbuf[c, j, f]), (tab_ci[j, 0, rows_of, :], tab_ci[j, 1, rows_of, :])
                )
                acc[f, j] = value if c == 0 else acc[f, j] + value

    @pl.loop(0, rows // ROWS16)
    def _(i):
        at = pl.ds(pl.multiple_of(i * ROWS16, ROWS16), ROWS16)
        for f in range(2):
            values = [(acc[f, 0, at, :block], None)]
            values += [(acc[f, j, at, :block], acc[f, j, at, block:]) for j in range(1, GROUP)]
            values += [(acc[f, 0, at, block:], None)]
            for a, value in enumerate(real_inverse(values)):
                out[0, f, at, a * block:(a + 1) * block] = value

    @pl.loop(1, n)
    def _(off):
        sums_copy((me + off) % n, me).wait_send()
        for c in range(2):
            forward_copy(c, (me + off) % n, me).wait_send()

    @pl.loop(1, GROUP)
    def _(off):
        for c in range(2):
            return_copy(c, peer(off), mine).wait_send()


def on_device(n, density, lens_weight, bin_distance, plane_bin, source_plane):
    planes, rows, cols = density.shape
    total_rows = rows * n
    block, xblock = cols // RADIX, total_rows // RADIX
    col_fwd, col_inv = column_tables(total_rows, cols)
    row_fwd, row_inv = row_tables(total_rows)
    tables = [jnp.asarray(t) for t in (col_fwd, row_fwd, row_inv, col_inv)]
    smem = pl.BlockSpec(memory_space=pltpu.SMEM)
    anywhere = pl.BlockSpec(memory_space=pl.ANY)
    dma = pltpu.SemaphoreType.DMA
    return pl.pallas_call(
        functools.partial(kernel, n),
        out_shape=jax.ShapeDtypeStruct((1, 2, rows, cols), F32),
        in_specs=[anywhere, smem, smem, smem, smem, anywhere, anywhere, anywhere, anywhere],
        out_specs=pl.BlockSpec(memory_space=pltpu.VMEM),
        scratch_shapes=[
            pltpu.VMEM((planes, rows, cols), BF16),
            pltpu.VMEM(col_fwd.shape, BF16),
            pltpu.VMEM(col_inv.shape, BF16),
            pltpu.VMEM(row_fwd.shape, BF16),
            pltpu.VMEM(row_inv.shape, BF16),
            pltpu.VMEM((planes, block), F32),
            pltpu.VMEM((n, planes, block), F32),
            pltpu.VMEM((GROUP, rows, 2 * block), F32),
            pltpu.VMEM((2, GROUP, rows, block), F32),
            pltpu.VMEM((2, total_rows, block), F32),
            pltpu.VMEM((RADIX, xblock, block), F32),
            pltpu.VMEM((RADIX, xblock, block), F32),
            pltpu.VMEM((RADIX, xblock, 2 * block), F32),
            pltpu.VMEM((2, 2, total_rows, block), F32),
            pltpu.VMEM((2, GROUP, 2, rows, block), F32),
            pltpu.VMEM((2, GROUP, rows, 2 * block), F32),
            dma((planes + 4,)),
            dma((n,)),
            dma((n,)),
            dma((2, n)),
            dma((2, n)),
            dma((2, GROUP)),
            dma((2, GROUP)),
            dma((4,)),
        ],
        compiler_params=pltpu.CompilerParams(
            collective_id=0, has_side_effects=True, vmem_limit_bytes=56 * 2**20
        ),
    )(density, lens_weight, bin_distance, plane_bin, source_plane, tables[0], tables[3], tables[1], tables[2])


def solution(mesh):
    return jax.shard_map(
        functools.partial(on_device, mesh.shape["rows"]),
        mesh=mesh,
        in_specs=(P("map", "rows", None), P(), P(), P(), P()),
        out_specs=P("map", None, "rows", None),
        check_vma=False,
    )
```

```python
import functools

import jax
import jax.numpy as jnp
import ml_dtypes
import numpy as np
from jax import lax
from jax.experimental import pallas as pl
from jax.experimental.pallas import tpu as pltpu
from jax.sharding import PartitionSpec as P

RADIX = 16
GROUP = RADIX // 2
EARLY, MIDDLE = 7, 8
ROWS16 = 16
MESH = pl.DeviceIdType.MESH
F32 = jnp.float32
BF16 = jnp.bfloat16


def split_table(table):
    high = table.astype(ml_dtypes.bfloat16)
    low = (table - high.astype(np.float64)).astype(ml_dtypes.bfloat16)
    return np.stack([high, low], axis=1)


def column_tables(total_rows, total_cols):
    block = total_cols // RADIX
    half = block // 2
    inside = np.arange(block)
    forward = np.zeros((GROUP, 2 * block, 2 * block))
    inverse = np.zeros((GROUP, 2 * block, 2 * block))
    for j in range(GROUP):
        for c in range(2):
            k = c * half + np.arange(half)
            freq = GROUP * k if j == 0 else j + RADIX * k
            angle = 2 * np.pi * ((inside[:, None] * freq[None, :]) % total_cols) / total_cols
            cos, sin = np.cos(angle), np.sin(angle)
            real = slice(c * block, c * block + half)
            imag = slice(c * block + half, (c + 1) * block)
            if j == 0:
                even = (k % 2 == 0)[None, :]
                cos_both = np.concatenate([np.where(even, cos, 0.0), np.where(even, 0.0, cos)])
                sin_both = np.concatenate([np.where(even, sin, 0.0), np.where(even, 0.0, sin)])
                fwd_re, fwd_im = cos_both, -sin_both
                inv_re, inv_im = 2 * cos_both, -2 * sin_both
                if c == 0:
                    sign = np.concatenate([(-1.0) ** inside, np.zeros(block)])
                    fwd_im[:, 0] = sign
                    inv_re[:, 0] = cos_both[:, 0]
                    inv_im[:, 0] = sign
            else:
                fwd_re = np.concatenate([cos, sin])
                fwd_im = np.concatenate([-sin, cos])
                inv_re = np.concatenate([cos, sin])
                inv_im = np.concatenate([-sin, cos])
            forward[j][:, real] = fwd_re
            forward[j][:, imag] = fwd_im
            inverse[j][real, :] = inv_re.T
            inverse[j][imag, :] = inv_im.T
    return split_table(forward), split_table(inverse / (total_rows * total_cols))


def row_tables(total_rows):
    block = total_rows // RADIX
    inside = np.arange(block)
    forward, inverse = [], []
    for k1 in range(RADIX):
        freq = k1 + RADIX * inside
        angle = 2 * np.pi * ((freq[:, None] * inside[None, :]) % total_rows) / total_rows
        cos, sin = np.cos(angle), np.sin(angle)
        forward.append(np.concatenate([cos, -sin], axis=1))
        inverse.append(np.concatenate([cos.T, sin.T], axis=1))
    return split_table(np.stack(forward)), split_table(np.stack(inverse))


def scaled(number, value):
    return value if number == 1.0 else (-value if number == -1.0 else value * np.float32(number))


def plus_of(a, b):
    return b if a is None else (a if b is None else a + b)


def minus_of(a, b):
    return a if b is None else (-b if a is None else a - b)


def rotate(value, step, length, orient):
    re, im = value
    if step == 0:
        return value
    cos, sin = np.cos(2 * np.pi * step / length), orient * np.sin(2 * np.pi * step / length)
    if 4 * step == length:
        return (None if im is None else -sin * im, sin * re)
    if im is None:
        return (re * np.float32(cos), re * np.float32(sin))
    return (
        re * np.float32(cos) - im * np.float32(sin),
        re * np.float32(sin) + im * np.float32(cos),
    )


def real_forward(values):
    n = len(values)
    if n == 1:
        return [(values[0], None)]
    even, odd = real_forward(values[0::2]), real_forward(values[1::2])
    out = [None] * (n // 2 + 1)
    for k in range(n // 4 + 1):
        turned = rotate(odd[k], k, n, -1.0)
        out[k] = (plus_of(even[k][0], turned[0]), plus_of(even[k][1], turned[1]))
        other = minus_of(turned[1], even[k][1])
        out[n // 2 - k] = (minus_of(even[k][0], turned[0]), other)
        if 4 * k == n:
            out[k] = (even[k][0], minus_of(None, odd[k][0]))
    return out


def real_inverse(values):
    n = 2 * (len(values) - 1)
    if n == 2:
        a, b = values[0][0], values[1][0]
        return [a + b, a - b]
    even, odd = [], []
    for k in range(n // 4 + 1):
        a, b = values[k], values[n // 2 - k]
        if k == 0 or 4 * k == n:
            if k == 0:
                even.append((a[0] + b[0], None))
                odd.append((a[0] - b[0], None))
            else:
                even.append((2.0 * a[0], None))
                odd.append((-2.0 * a[1], None))
            continue
        even.append((a[0] + b[0], a[1] - b[1]))
        odd.append(rotate((a[0] - b[0], a[1] + b[1]), k, n, 1.0))
    out = [None] * n
    out[0::2] = real_inverse(even)
    out[1::2] = real_inverse(odd)
    return out


def times_i(value, sign):
    return pltpu.roll(value, value.shape[1] // 2, 1) * sign


def packed_dft(values, orient, sign):
    n = len(values)
    if n == 1:
        return values
    even, odd = packed_dft(values[0::2], orient, sign), packed_dft(values[1::2], orient, sign)
    out = [None] * n
    for k in range(n // 2):
        value = odd[k]
        if 4 * k == n:
            value = times_i(value, sign) * np.float32(orient)
        elif k:
            angle = 2 * np.pi * k / n
            value = value * np.float32(np.cos(angle)) + times_i(value, sign) * np.float32(
                orient * np.sin(angle)
            )
        out[k] = even[k] + value
        out[k + n // 2] = even[k] - value
    return out


def halves(value):
    high = value.astype(BF16)
    return high, (value - high.astype(F32)).astype(BF16)


def product(a, b):
    def dot(x, y):
        return jnp.dot(x, y, preferred_element_type=F32)

    return dot(a[0], b[0]) + dot(a[0], b[1]) + dot(a[1], b[0])


def frequency(positions, length):
    return jnp.where(positions < length // 2, positions, positions - length).astype(F32) / length


def kernel(
    n, density, weight, bins, plane_bin, source, col_fwd, col_inv, row_fwd, row_inv, out,
    dens, tab_cf, tab_ci, tab_rf, tab_ri, part, sums, parts, sbuf, xin, zbuf, zconj, wbuf, gbuf,
    rbuf, acc, load_sem, send_m, recv_m, send_f, recv_f, send_r, recv_r, own_sem,
):
    planes, rows, cols = density.shape
    total_rows = rows * n
    block = cols // RADIX
    half = block // 2
    xblock = total_rows // RADIX
    me = lax.axis_index("rows")
    group = me // GROUP
    mine = me % GROUP

    loads = [pltpu.make_async_copy(density.at[l], dens.at[l], load_sem.at[l]) for l in range(planes)]
    for at, (src, dst) in enumerate(
        [(col_fwd, tab_cf), (row_fwd, tab_rf), (row_inv, tab_ri), (col_inv, tab_ci)]
    ):
        loads.append(pltpu.make_async_copy(src, dst, load_sem.at[planes + at]))
    for load in loads[:planes]:
        load.start()

    barrier = pltpu.get_barrier_semaphore()

    @pl.loop(1, n)
    def _(off):
        pl.semaphore_signal(
            barrier, inc=1, device_id={"rows": (me + off) % n}, device_id_type=MESH
        )

    for l in range(planes):
        loads[l].wait()

        def add_rows(i, total, l=l):
            at = pl.ds(pl.multiple_of(i * ROWS16, ROWS16), ROWS16)
            pieces = [dens[l, at, a * block:(a + 1) * block].astype(F32) for a in range(RADIX)]
            while len(pieces) > 1:
                pieces = [x + y for x, y in zip(pieces[0::2], pieces[1::2])]
            return total + pieces[0]

        total = lax.fori_loop(0, rows // ROWS16, add_rows, jnp.zeros((ROWS16, block), F32))
        part[l:l + 1, :] = jnp.sum(total, axis=0, keepdims=True)

    for load in loads[planes:]:
        load.start()

    pl.semaphore_wait(barrier, n - 1)

    def sums_copy(dst, slot):
        return pltpu.make_async_remote_copy(
            src_ref=part, dst_ref=sums.at[slot], send_sem=send_m.at[dst], recv_sem=recv_m.at[slot],
            device_id={"rows": dst}, device_id_type=MESH,
        )

    @pl.loop(1, n)
    def _(off):
        sums_copy((me + off) % n, me).start()

    sums[me] = part[...]

    @pl.loop(1, n)
    def _(off):
        sums_copy((me + off) % n, (me + off) % n).wait_recv()

    cells = np.float32(total_rows * cols)
    whole = jnp.sum(jnp.sum(sums[...], axis=0), axis=1, keepdims=True)
    mean = jnp.broadcast_to(whole / cells, (planes, block))
    source_plane = source[0]
    source_distance = jnp.full((1, block), bins[plane_bin[source_plane]], F32)
    scales, offset = [], None
    for l in range(planes):
        distance = jnp.full((1, block), bins[plane_bin[l]], F32)
        lens = jnp.full((1, block), jnp.where(l <= source_plane, weight[l], np.float32(0.0)), F32)
        coefficient = lens * (1.0 - distance / source_distance)
        scales.append(coefficient / mean[l:l + 1, :])
        offset = coefficient if offset is None else offset + coefficient

    @pl.loop(0, rows // ROWS16)
    def _(i):
        at = pl.ds(pl.multiple_of(i * ROWS16, ROWS16), ROWS16)
        values = []
        for a in range(RADIX):
            value = None
            for l in range(planes):
                term = dens[l, at, a * block:(a + 1) * block].astype(F32) * scales[l]
                value = term if value is None else value + term
            values.append(value - offset)
        spectrum = real_forward(values)
        parts[0, at, :block] = spectrum[0][0]
        parts[0, at, block:] = spectrum[GROUP][0]
        for j in range(1, GROUP):
            parts[j, at, :block] = spectrum[j][0]
            parts[j, at, block:] = spectrum[j][1]

    loads[planes].wait()

    def forward_copy(c, dst, slot):
        return pltpu.make_async_remote_copy(
            src_ref=sbuf.at[c, dst % GROUP],
            dst_ref=xin.at[c, pl.ds(pl.multiple_of(slot * rows, rows), rows)],
            send_sem=send_f.at[c, dst], recv_sem=recv_f.at[c, slot],
            device_id={"rows": dst}, device_id_type=MESH,
        )

    def forward_own(c):
        return pltpu.make_async_copy(
            sbuf.at[c, mine], xin.at[c, pl.ds(pl.multiple_of(me * rows, rows), rows)],
            own_sem.at[c],
        )

    def peer(off):
        return group * GROUP + (mine + off) % GROUP

    def send_across(c, i):
        for far in range(1, n // GROUP):
            dst = (group + far) % (n // GROUP) * GROUP + (mine + i) % GROUP
            forward_copy(c, dst, me).start()

    early, middle = EARLY, MIDDLE

    for c in range(2):
        lanes = slice(c * block, (c + 1) * block)

        @pl.loop(0, GROUP, unroll=4)
        def _(j, c=c, lanes=lanes):
            sbuf[c, j] = product(halves(parts[j]), (tab_cf[j, 0, :, lanes], tab_cf[j, 1, :, lanes]))

        forward_own(c).start()
        if c == 0:
            @pl.loop(0, GROUP)
            def _(i):
                send_across(0, i)

                @pl.when(i > 0)
                def _():
                    forward_copy(0, peer(i), me).start()
        else:
            @pl.loop(1, GROUP)
            def _(i):
                forward_copy(1, peer(i), me).start()

                @pl.when(i <= early)
                def _():
                    send_across(1, i - 1)

    lane = lax.broadcasted_iota(jnp.int32, (1, block), 1)
    sign = jnp.where(lane < half, np.float32(-1.0), np.float32(1.0))
    loads[planes + 1].wait()
    loads[planes + 2].wait()
    loads[planes + 3].wait()

    def return_copy(c, dst, slot):
        return pltpu.make_async_remote_copy(
            src_ref=gbuf.at[c, :, pl.ds(pl.multiple_of(dst * rows, rows), rows)],
            dst_ref=rbuf.at[c, slot],
            send_sem=send_r.at[c, dst % GROUP], recv_sem=recv_r.at[c, slot],
            device_id={"rows": dst}, device_id_type=MESH,
        )

    def return_own(c):
        return pltpu.make_async_copy(
            gbuf.at[c, :, pl.ds(pl.multiple_of(me * rows, rows), rows)], rbuf.at[c, mine],
            own_sem.at[2 + c],
        )

    for c in range(2):
        forward_own(c).wait()

        @pl.loop(1, n)
        def _(off, c=c):
            forward_copy(c, (me + off) % n, (me + off) % n).wait_recv()

        def first_pass(target, conjugate, c=c):
            @pl.loop(0, xblock // ROWS16)
            def _(i):
                at = pl.multiple_of(i * ROWS16, ROWS16)
                values = [xin[c, pl.ds(at + a * xblock, ROWS16), :] for a in range(RADIX)]
                if conjugate:
                    values = [-sign * value for value in values]
                for k1, value in enumerate(packed_dft(values, -1.0, sign)):
                    target[k1, pl.ds(at, ROWS16), :] = value

        first_pass(zbuf, False)
        if c == 0:
            first_pass(zconj, True)

        @pl.loop(0, RADIX, unroll=4)
        def _(k1, c=c):
            def transform(value):
                stacked = jnp.concatenate([value, times_i(value, sign)], axis=0)
                return product((tab_rf[k1, 0], tab_rf[k1, 1]), halves(stacked))

            spectrum = transform(zbuf[k1])
            turned = times_i(spectrum, sign)
            shape = (xblock, block)
            kx = k1 + RADIX * lax.broadcasted_iota(jnp.int32, shape, 0)
            q = lax.broadcasted_iota(jnp.int32, shape, 1) % half
            k2 = c * half + q
            ky = jnp.where(mine == 0, GROUP * k2, mine + RADIX * k2)
            fx, fy = frequency(kx, total_rows), frequency(ky, cols)
            squared = fx * fx + fy * fy
            recip = 1.0 / jnp.where(squared > 0, squared, np.float32(1.0))
            plus = (fx * fx - fy * fy) * recip
            cross = 2.0 * fx * fy * recip
            nyquist = kx == total_rows // 2
            zero = jnp.zeros(shape, F32)
            direct, across = plus, jnp.where(nyquist, cross, zero)
            second = jnp.where(nyquist, zero, cross) * spectrum
            if c == 0:
                mirrored = transform(zconj[k1])
                packed = jnp.logical_and(q == 0, mine == 0)
                recip_n = 1.0 / (fx * fx + np.float32(0.25))
                plus_n = (fx * fx - np.float32(0.25)) * recip_n
                cross_n = -fx * recip_n
                odd_n = jnp.where(nyquist, zero, cross_n)
                even_n = jnp.where(nyquist, cross_n, zero)
                mirror_direct = jnp.where(packed, 0.5 * (plus - plus_n), zero)
                mirror_across = jnp.where(packed, -0.5 * odd_n, zero)
                direct = jnp.where(packed, 0.5 * (plus + plus_n), direct)
                across = jnp.where(packed, 0.5 * odd_n, across)
                second = jnp.where(packed, 0.5 * even_n * (spectrum - mirrored), second)
                first = (
                    direct * spectrum + across * turned
                    + mirror_direct * mirrored + mirror_across * times_i(mirrored, sign)
                )
            else:
                first = direct * spectrum + across * turned
            both = jnp.concatenate(
                [
                    jnp.concatenate([first, times_i(first, sign)], axis=0),
                    jnp.concatenate([second, times_i(second, sign)], axis=0),
                ],
                axis=1,
            )
            wbuf[k1] = product((tab_ri[k1, 0], tab_ri[k1, 1]), halves(both))

        if c == 0:
            for i in range(early, middle):
                send_across(1, i)

        @pl.loop(0, xblock // ROWS16)
        def _(i, c=c):
            at = pl.multiple_of(i * ROWS16, ROWS16)
            for f in range(2):
                values = [
                    wbuf[k1, pl.ds(at, ROWS16), f * block:(f + 1) * block] for k1 in range(RADIX)
                ]
                for a, value in enumerate(packed_dft(values, 1.0, sign)):
                    gbuf[c, f, pl.ds(at + a * xblock, ROWS16), :] = value

        return_own(c).start()

        @pl.loop(1, GROUP)
        def _(off, c=c):
            return_copy(c, peer(off), mine).start()
            if c == 0:
                @pl.when(off < GROUP - middle + 1)
                def _():
                    send_across(1, middle + off - 1)

    for c in range(2):
        return_own(c).wait()

        @pl.loop(1, GROUP)
        def _(off, c=c):
            return_copy(c, peer(off), (mine + off) % GROUP).wait_recv()

        rows_of = slice(c * block, (c + 1) * block)

        @pl.loop(0, GROUP, unroll=4)
        def _(j, c=c, rows_of=rows_of):
            for f in range(2):
                value = product(
                    halves(rbuf[c, j, f]), (tab_ci[j, 0, rows_of, :], tab_ci[j, 1, rows_of, :])
                )
                acc[f, j] = value if c == 0 else acc[f, j] + value

    @pl.loop(0, rows // ROWS16)
    def _(i):
        at = pl.ds(pl.multiple_of(i * ROWS16, ROWS16), ROWS16)
        for f in range(2):
            values = [(acc[f, 0, at, :block], None)]
            values += [(acc[f, j, at, :block], acc[f, j, at, block:]) for j in range(1, GROUP)]
            values += [(acc[f, 0, at, block:], None)]
            for a, value in enumerate(real_inverse(values)):
                out[0, f, at, a * block:(a + 1) * block] = value

    @pl.loop(1, n)
    def _(off):
        sums_copy((me + off) % n, me).wait_send()
        for c in range(2):
            forward_copy(c, (me + off) % n, me).wait_send()

    @pl.loop(1, GROUP)
    def _(off):
        for c in range(2):
            return_copy(c, peer(off), mine).wait_send()


def on_device(n, density, lens_weight, bin_distance, plane_bin, source_plane):
    planes, rows, cols = density.shape
    total_rows = rows * n
    block, xblock = cols // RADIX, total_rows // RADIX
    col_fwd, col_inv = column_tables(total_rows, cols)
    row_fwd, row_inv = row_tables(total_rows)
    tables = [jnp.asarray(t) for t in (col_fwd, row_fwd, row_inv, col_inv)]
    smem = pl.BlockSpec(memory_space=pltpu.SMEM)
    anywhere = pl.BlockSpec(memory_space=pl.ANY)
    dma = pltpu.SemaphoreType.DMA
    return pl.pallas_call(
        functools.partial(kernel, n),
        out_shape=pltpu.VMEM((1, 2, rows, cols), F32),
        in_specs=[anywhere, smem, smem, smem, smem, anywhere, anywhere, anywhere, anywhere],
        out_specs=pl.BlockSpec(memory_space=pltpu.VMEM),
        scratch_shapes=[
            pltpu.VMEM((planes, rows, cols), BF16),
            pltpu.VMEM(col_fwd.shape, BF16),
            pltpu.VMEM(col_inv.shape, BF16),
            pltpu.VMEM(row_fwd.shape, BF16),
            pltpu.VMEM(row_inv.shape, BF16),
            pltpu.VMEM((planes, block), F32),
            pltpu.VMEM((n, planes, block), F32),
            pltpu.VMEM((GROUP, rows, 2 * block), F32),
            pltpu.VMEM((2, GROUP, rows, block), F32),
            pltpu.VMEM((2, total_rows, block), F32),
            pltpu.VMEM((RADIX, xblock, block), F32),
            pltpu.VMEM((RADIX, xblock, block), F32),
            pltpu.VMEM((RADIX, xblock, 2 * block), F32),
            pltpu.VMEM((2, 2, total_rows, block), F32),
            pltpu.VMEM((2, GROUP, 2, rows, block), F32),
            pltpu.VMEM((2, GROUP, rows, 2 * block), F32),
            dma((planes + 4,)),
            dma((n,)),
            dma((n,)),
            dma((2, n)),
            dma((2, n)),
            dma((2, GROUP)),
            dma((2, GROUP)),
            dma((4,)),
        ],
        compiler_params=pltpu.CompilerParams(
            collective_id=0, has_side_effects=True, vmem_limit_bytes=56 * 2**20
        ),
    )(density, lens_weight, bin_distance, plane_bin, source_plane, tables[0], tables[3], tables[1], tables[2])


def solution(mesh):
    return jax.shard_map(
        functools.partial(on_device, mesh.shape["rows"]),
        mesh=mesh,
        in_specs=(P("map", "rows", None), P(), P(), P(), P()),
        out_specs=P("map", None, "rows", None),
        check_vma=False,
    )
```

```python
import functools

import jax
import jax.numpy as jnp
import ml_dtypes
import numpy as np
from jax import lax
from jax.experimental import pallas as pl
from jax.experimental.pallas import tpu as pltpu
from jax.sharding import PartitionSpec as P

RADIX = 16
GROUP = RADIX // 2
EARLY, MIDDLE = 7, 8
ROWS16 = 16
MESH = pl.DeviceIdType.MESH
F32 = jnp.float32
BF16 = jnp.bfloat16


def split_table(table):
    high = table.astype(ml_dtypes.bfloat16)
    low = (table - high.astype(np.float64)).astype(ml_dtypes.bfloat16)
    return np.stack([high, low], axis=1)


def column_tables(total_rows, total_cols):
    block = total_cols // RADIX
    half = block // 2
    inside = np.arange(block)
    forward = np.zeros((GROUP, 2 * block, 2 * block))
    inverse = np.zeros((GROUP, 2 * block, 2 * block))
    for j in range(GROUP):
        for c in range(2):
            k = c * half + np.arange(half)
            freq = GROUP * k if j == 0 else j + RADIX * k
            angle = 2 * np.pi * ((inside[:, None] * freq[None, :]) % total_cols) / total_cols
            cos, sin = np.cos(angle), np.sin(angle)
            real = slice(c * block, c * block + half)
            imag = slice(c * block + half, (c + 1) * block)
            if j == 0:
                even = (k % 2 == 0)[None, :]
                cos_both = np.concatenate([np.where(even, cos, 0.0), np.where(even, 0.0, cos)])
                sin_both = np.concatenate([np.where(even, sin, 0.0), np.where(even, 0.0, sin)])
                fwd_re, fwd_im = cos_both, -sin_both
                inv_re, inv_im = 2 * cos_both, -2 * sin_both
                if c == 0:
                    sign = np.concatenate([(-1.0) ** inside, np.zeros(block)])
                    fwd_im[:, 0] = sign
                    inv_re[:, 0] = cos_both[:, 0]
                    inv_im[:, 0] = sign
            else:
                fwd_re = np.concatenate([cos, sin])
                fwd_im = np.concatenate([-sin, cos])
                inv_re = np.concatenate([cos, sin])
                inv_im = np.concatenate([-sin, cos])
            forward[j][:, real] = fwd_re
            forward[j][:, imag] = fwd_im
            inverse[j][real, :] = inv_re.T
            inverse[j][imag, :] = inv_im.T
    return split_table(forward), split_table(inverse / (total_rows * total_cols))


def row_tables(total_rows):
    block = total_rows // RADIX
    inside = np.arange(block)
    forward, inverse = [], []
    for k1 in range(RADIX):
        freq = k1 + RADIX * inside
        angle = 2 * np.pi * ((freq[:, None] * inside[None, :]) % total_rows) / total_rows
        cos, sin = np.cos(angle), np.sin(angle)
        forward.append(np.concatenate([cos, -sin], axis=1))
        inverse.append(np.concatenate([cos.T, sin.T], axis=1))
    return split_table(np.stack(forward)), split_table(np.stack(inverse))


def scaled(number, value):
    return value if number == 1.0 else (-value if number == -1.0 else value * np.float32(number))


def plus_of(a, b):
    return b if a is None else (a if b is None else a + b)


def minus_of(a, b):
    return a if b is None else (-b if a is None else a - b)


def rotate(value, step, length, orient):
    re, im = value
    if step == 0:
        return value
    cos, sin = np.cos(2 * np.pi * step / length), orient * np.sin(2 * np.pi * step / length)
    if 4 * step == length:
        return (None if im is None else -sin * im, sin * re)
    if im is None:
        return (re * np.float32(cos), re * np.float32(sin))
    return (
        re * np.float32(cos) - im * np.float32(sin),
        re * np.float32(sin) + im * np.float32(cos),
    )


def real_forward(values):
    n = len(values)
    if n == 1:
        return [(values[0], None)]
    even, odd = real_forward(values[0::2]), real_forward(values[1::2])
    out = [None] * (n // 2 + 1)
    for k in range(n // 4 + 1):
        turned = rotate(odd[k], k, n, -1.0)
        out[k] = (plus_of(even[k][0], turned[0]), plus_of(even[k][1], turned[1]))
        other = minus_of(turned[1], even[k][1])
        out[n // 2 - k] = (minus_of(even[k][0], turned[0]), other)
        if 4 * k == n:
            out[k] = (even[k][0], minus_of(None, odd[k][0]))
    return out


def real_inverse(values):
    n = 2 * (len(values) - 1)
    if n == 2:
        a, b = values[0][0], values[1][0]
        return [a + b, a - b]
    even, odd = [], []
    for k in range(n // 4 + 1):
        a, b = values[k], values[n // 2 - k]
        if k == 0 or 4 * k == n:
            if k == 0:
                even.append((a[0] + b[0], None))
                odd.append((a[0] - b[0], None))
            else:
                even.append((2.0 * a[0], None))
                odd.append((-2.0 * a[1], None))
            continue
        even.append((a[0] + b[0], a[1] - b[1]))
        odd.append(rotate((a[0] - b[0], a[1] + b[1]), k, n, 1.0))
    out = [None] * n
    out[0::2] = real_inverse(even)
    out[1::2] = real_inverse(odd)
    return out


def times_i(value, sign):
    return pltpu.roll(value, value.shape[1] // 2, 1) * sign


def packed_dft(values, orient, sign):
    n = len(values)
    if n == 1:
        return values
    even, odd = packed_dft(values[0::2], orient, sign), packed_dft(values[1::2], orient, sign)
    out = [None] * n
    for k in range(n // 2):
        value = odd[k]
        if 4 * k == n:
            value = times_i(value, sign) * np.float32(orient)
        elif k:
            angle = 2 * np.pi * k / n
            value = value * np.float32(np.cos(angle)) + times_i(value, sign) * np.float32(
                orient * np.sin(angle)
            )
        out[k] = even[k] + value
        out[k + n // 2] = even[k] - value
    return out


def halves(value):
    high = value.astype(BF16)
    return high, (value - high.astype(F32)).astype(BF16)


def product(a, b):
    def dot(x, y):
        return jnp.dot(x, y, preferred_element_type=F32)

    return dot(a[0], b[0]) + dot(a[0], b[1]) + dot(a[1], b[0])


def frequency(positions, length):
    return jnp.where(positions < length // 2, positions, positions - length).astype(F32) / length


def kernel(
    n, density, weight, bins, plane_bin, source, col_fwd, col_inv, row_fwd, row_inv, out,
    dens, tab_cf, tab_ci, tab_rf, tab_ri, part, sums, parts, sbuf, xin, zbuf, wbuf, gbuf,
    rbuf, acc, load_sem, send_m, recv_m, send_f, recv_f, send_r, recv_r, own_sem,
):
    planes, rows, cols = density.shape
    total_rows = rows * n
    block = cols // RADIX
    half = block // 2
    xblock = total_rows // RADIX
    me = lax.axis_index("rows")
    group = me // GROUP
    mine = me % GROUP

    loads = [pltpu.make_async_copy(density.at[l], dens.at[l], load_sem.at[l]) for l in range(planes)]
    for at, (src, dst) in enumerate(
        [(col_fwd, tab_cf), (row_fwd, tab_rf), (row_inv, tab_ri), (col_inv, tab_ci)]
    ):
        loads.append(pltpu.make_async_copy(src, dst, load_sem.at[planes + at]))
    for load in loads[:planes]:
        load.start()

    barrier = pltpu.get_barrier_semaphore()

    @pl.loop(1, n)
    def _(off):
        pl.semaphore_signal(
            barrier, inc=1, device_id={"rows": (me + off) % n}, device_id_type=MESH
        )

    for l in range(planes):
        loads[l].wait()

        def add_rows(i, total, l=l):
            at = pl.ds(pl.multiple_of(i * ROWS16, ROWS16), ROWS16)
            pieces = [dens[l, at, a * block:(a + 1) * block].astype(F32) for a in range(RADIX)]
            while len(pieces) > 1:
                pieces = [x + y for x, y in zip(pieces[0::2], pieces[1::2])]
            return total + pieces[0]

        total = lax.fori_loop(0, rows // ROWS16, add_rows, jnp.zeros((ROWS16, block), F32))
        part[l:l + 1, :] = jnp.sum(total, axis=0, keepdims=True)

    for load in loads[planes:]:
        load.start()

    pl.semaphore_wait(barrier, n - 1)

    def sums_copy(dst, slot):
        return pltpu.make_async_remote_copy(
            src_ref=part, dst_ref=sums.at[slot], send_sem=send_m.at[dst], recv_sem=recv_m.at[slot],
            device_id={"rows": dst}, device_id_type=MESH,
        )

    @pl.loop(1, n)
    def _(off):
        sums_copy((me + off) % n, me).start()

    sums[me] = part[...]

    @pl.loop(1, n)
    def _(off):
        sums_copy((me + off) % n, (me + off) % n).wait_recv()

    cells = np.float32(total_rows * cols)
    whole = jnp.sum(jnp.sum(sums[...], axis=0), axis=1, keepdims=True)
    mean = jnp.broadcast_to(whole / cells, (planes, block))
    source_plane = source[0]
    source_distance = jnp.full((1, block), bins[plane_bin[source_plane]], F32)
    scales, offset = [], None
    for l in range(planes):
        distance = jnp.full((1, block), bins[plane_bin[l]], F32)
        lens = jnp.full((1, block), jnp.where(l <= source_plane, weight[l], np.float32(0.0)), F32)
        coefficient = lens * (1.0 - distance / source_distance)
        scales.append(coefficient / mean[l:l + 1, :])
        offset = coefficient if offset is None else offset + coefficient

    @pl.loop(0, rows // ROWS16)
    def _(i):
        at = pl.ds(pl.multiple_of(i * ROWS16, ROWS16), ROWS16)
        values = []
        for a in range(RADIX):
            value = None
            for l in range(planes):
                term = dens[l, at, a * block:(a + 1) * block].astype(F32) * scales[l]
                value = term if value is None else value + term
            values.append(value - offset)
        spectrum = real_forward(values)
        parts[0, at, :block] = spectrum[0][0]
        parts[0, at, block:] = spectrum[GROUP][0]
        for j in range(1, GROUP):
            parts[j, at, :block] = spectrum[j][0]
            parts[j, at, block:] = spectrum[j][1]

    loads[planes].wait()

    def forward_copy(c, dst, slot):
        return pltpu.make_async_remote_copy(
            src_ref=sbuf.at[c, dst % GROUP],
            dst_ref=xin.at[c, pl.ds(pl.multiple_of(slot * rows, rows), rows)],
            send_sem=send_f.at[c, dst], recv_sem=recv_f.at[c, slot],
            device_id={"rows": dst}, device_id_type=MESH,
        )

    def forward_own(c):
        return pltpu.make_async_copy(
            sbuf.at[c, mine], xin.at[c, pl.ds(pl.multiple_of(me * rows, rows), rows)],
            own_sem.at[c],
        )

    def peer(off):
        return group * GROUP + (mine + off) % GROUP

    def send_across(c, i):
        for far in range(1, n // GROUP):
            dst = (group + far) % (n // GROUP) * GROUP + (mine + i) % GROUP
            forward_copy(c, dst, me).start()

    early, middle = EARLY, MIDDLE

    for c in range(2):
        lanes = slice(c * block, (c + 1) * block)

        @pl.loop(0, GROUP, unroll=4)
        def _(j, c=c, lanes=lanes):
            sbuf[c, j] = product(halves(parts[j]), (tab_cf[j, 0, :, lanes], tab_cf[j, 1, :, lanes]))

        forward_own(c).start()
        if c == 0:
            @pl.loop(0, GROUP)
            def _(i):
                send_across(0, i)

                @pl.when(i > 0)
                def _():
                    forward_copy(0, peer(i), me).start()
        else:
            @pl.loop(1, GROUP)
            def _(i):
                forward_copy(1, peer(i), me).start()

                @pl.when(i <= early)
                def _():
                    send_across(1, i - 1)

    lane = lax.broadcasted_iota(jnp.int32, (1, block), 1)
    sign = jnp.where(lane < half, np.float32(-1.0), np.float32(1.0))
    loads[planes + 1].wait()
    loads[planes + 2].wait()
    loads[planes + 3].wait()

    def return_copy(c, f, dst, slot):
        return pltpu.make_async_remote_copy(
            src_ref=gbuf.at[c, f, pl.ds(pl.multiple_of(dst * rows, rows), rows)],
            dst_ref=rbuf.at[c, slot, f],
            send_sem=send_r.at[c, f, dst % GROUP], recv_sem=recv_r.at[c, f, slot],
            device_id={"rows": dst}, device_id_type=MESH,
        )

    def return_own(c, f):
        return pltpu.make_async_copy(
            gbuf.at[c, f, pl.ds(pl.multiple_of(me * rows, rows), rows)], rbuf.at[c, mine, f],
            own_sem.at[2 + 2 * c + f],
        )

    for c in range(2):
        forward_own(c).wait()

        @pl.loop(1, n)
        def _(off, c=c):
            forward_copy(c, (me + off) % n, (me + off) % n).wait_recv()

        def first_pass(target, c=c):
            @pl.loop(0, xblock // ROWS16)
            def _(i):
                at = pl.multiple_of(i * ROWS16, ROWS16)
                values = [xin[c, pl.ds(at + a * xblock, ROWS16), :] for a in range(RADIX)]
                for k1, value in enumerate(packed_dft(values, -1.0, sign)):
                    target[k1, pl.ds(at, ROWS16), :] = value

        first_pass(zbuf)

        @pl.loop(0, RADIX, unroll=8)
        def _(k1, c=c):
            def transform(value):
                stacked = jnp.concatenate([value, times_i(value, sign)], axis=0)
                return product((tab_rf[k1, 0], tab_rf[k1, 1]), halves(stacked))

            spectrum = transform(zbuf[k1])
            turned = times_i(spectrum, sign)
            shape = (xblock, block)
            kx = k1 + RADIX * lax.broadcasted_iota(jnp.int32, shape, 0)
            q = lax.broadcasted_iota(jnp.int32, shape, 1) % half
            k2 = c * half + q
            ky = jnp.where(mine == 0, GROUP * k2, mine + RADIX * k2)
            fx, fy = frequency(kx, total_rows), frequency(ky, cols)
            squared = fx * fx + fy * fy
            recip = 1.0 / jnp.where(squared > 0, squared, np.float32(1.0))
            plus = (fx * fx - fy * fy) * recip
            cross = 2.0 * fx * fy * recip
            nyquist = kx == total_rows // 2
            zero = jnp.zeros(shape, F32)
            direct, across = plus, jnp.where(nyquist, cross, zero)
            second = jnp.where(nyquist, zero, cross) * spectrum
            if c == 0:
                mirrored = transform(-sign * zbuf[(RADIX - k1) % RADIX])
                packed = jnp.logical_and(q == 0, mine == 0)
                recip_n = 1.0 / (fx * fx + np.float32(0.25))
                plus_n = (fx * fx - np.float32(0.25)) * recip_n
                cross_n = -fx * recip_n
                odd_n = jnp.where(nyquist, zero, cross_n)
                even_n = jnp.where(nyquist, cross_n, zero)
                mirror_direct = jnp.where(packed, 0.5 * (plus - plus_n), zero)
                mirror_across = jnp.where(packed, -0.5 * odd_n, zero)
                direct = jnp.where(packed, 0.5 * (plus + plus_n), direct)
                across = jnp.where(packed, 0.5 * odd_n, across)
                second = jnp.where(packed, 0.5 * even_n * (spectrum - mirrored), second)
                first = (
                    direct * spectrum + across * turned
                    + mirror_direct * mirrored + mirror_across * times_i(mirrored, sign)
                )
            else:
                first = direct * spectrum + across * turned
            both = jnp.concatenate(
                [
                    jnp.concatenate([first, times_i(first, sign)], axis=0),
                    jnp.concatenate([second, times_i(second, sign)], axis=0),
                ],
                axis=1,
            )
            wbuf[k1] = product((tab_ri[k1, 0], tab_ri[k1, 1]), halves(both))

        if c == 0:
            for i in range(early, middle):
                send_across(1, i)

        for f in range(2):
            @pl.loop(0, xblock // ROWS16)
            def _(i, c=c, f=f):
                at = pl.multiple_of(i * ROWS16, ROWS16)
                values = [
                    wbuf[k1, pl.ds(at, ROWS16), f * block:(f + 1) * block] for k1 in range(RADIX)
                ]
                for a, value in enumerate(packed_dft(values, 1.0, sign)):
                    gbuf[c, f, pl.ds(at + a * xblock, ROWS16), :] = value

            return_own(c, f).start()

            @pl.loop(1, GROUP)
            def _(off, c=c, f=f):
                return_copy(c, f, peer(off), mine).start()
                if c == 0 and f == 0:
                    @pl.when(off < GROUP - middle + 1)
                    def _():
                        send_across(1, middle + off - 1)

    for c in range(2):
        rows_of = slice(c * block, (c + 1) * block)
        for f in range(2):
            return_own(c, f).wait()

            @pl.loop(1, GROUP)
            def _(off, c=c, f=f):
                return_copy(c, f, peer(off), (mine + off) % GROUP).wait_recv()

            @pl.loop(0, GROUP, unroll=4)
            def _(j, c=c, f=f, rows_of=rows_of):
                value = product(
                    halves(rbuf[c, j, f]), (tab_ci[j, 0, rows_of, :], tab_ci[j, 1, rows_of, :])
                )
                acc[f, j] = value if c == 0 else acc[f, j] + value

    @pl.loop(0, rows // ROWS16)
    def _(i):
        at = pl.ds(pl.multiple_of(i * ROWS16, ROWS16), ROWS16)
        for f in range(2):
            values = [(acc[f, 0, at, :block], None)]
            values += [(acc[f, j, at, :block], acc[f, j, at, block:]) for j in range(1, GROUP)]
            values += [(acc[f, 0, at, block:], None)]
            for a, value in enumerate(real_inverse(values)):
                out[0, f, at, a * block:(a + 1) * block] = value

    @pl.loop(1, n)
    def _(off):
        sums_copy((me + off) % n, me).wait_send()
        for c in range(2):
            forward_copy(c, (me + off) % n, me).wait_send()

    @pl.loop(1, GROUP)
    def _(off):
        for c in range(2):
            for f in range(2):
                return_copy(c, f, peer(off), mine).wait_send()


def on_device(n, density, lens_weight, bin_distance, plane_bin, source_plane):
    planes, rows, cols = density.shape
    total_rows = rows * n
    block, xblock = cols // RADIX, total_rows // RADIX
    col_fwd, col_inv = column_tables(total_rows, cols)
    row_fwd, row_inv = row_tables(total_rows)
    tables = [jnp.asarray(t) for t in (col_fwd, row_fwd, row_inv, col_inv)]
    smem = pl.BlockSpec(memory_space=pltpu.SMEM)
    anywhere = pl.BlockSpec(memory_space=pl.ANY)
    dma = pltpu.SemaphoreType.DMA
    return pl.pallas_call(
        functools.partial(kernel, n),
        out_shape=pltpu.VMEM((1, 2, rows, cols), F32),
        in_specs=[anywhere, smem, smem, smem, smem, anywhere, anywhere, anywhere, anywhere],
        out_specs=pl.BlockSpec(memory_space=pltpu.VMEM),
        scratch_shapes=[
            pltpu.VMEM((planes, rows, cols), BF16),
            pltpu.VMEM(col_fwd.shape, BF16),
            pltpu.VMEM(col_inv.shape, BF16),
            pltpu.VMEM(row_fwd.shape, BF16),
            pltpu.VMEM(row_inv.shape, BF16),
            pltpu.VMEM((planes, block), F32),
            pltpu.VMEM((n, planes, block), F32),
            pltpu.VMEM((GROUP, rows, 2 * block), F32),
            pltpu.VMEM((2, GROUP, rows, block), F32),
            pltpu.VMEM((2, total_rows, block), F32),
            pltpu.VMEM((RADIX, xblock, block), F32),
            pltpu.VMEM((RADIX, xblock, 2 * block), F32),
            pltpu.VMEM((2, 2, total_rows, block), F32),
            pltpu.VMEM((2, GROUP, 2, rows, block), F32),
            pltpu.VMEM((2, GROUP, rows, 2 * block), F32),
            dma((planes + 4,)),
            dma((n,)),
            dma((n,)),
            dma((2, n)),
            dma((2, n)),
            dma((2, 2, GROUP)),
            dma((2, 2, GROUP)),
            dma((6,)),
        ],
        compiler_params=pltpu.CompilerParams(
            collective_id=0, has_side_effects=True, vmem_limit_bytes=56 * 2**20
        ),
    )(density, lens_weight, bin_distance, plane_bin, source_plane, tables[0], tables[3], tables[1], tables[2])


def solution(mesh):
    return jax.shard_map(
        functools.partial(on_device, mesh.shape["rows"]),
        mesh=mesh,
        in_specs=(P("map", "rows", None), P(), P(), P(), P()),
        out_specs=P("map", None, "rows", None),
        check_vma=False,
    )
```
